32 devices in a mesh: group: 2 (over y), expert: 4 (over z), tensor: 2 (over x), pipe: 2 (over core).
Axes of the slice: x: 2, y: 2, z: 4, core: 2. Of those that a mesh axis runs over, the one named last changes fastest.
Arguments:
- attn_terms: bfloat16 [2, 320, 3584], P('tensor', ('group', 'expert')), parts along dimension 1, may hold values from -4 to 4
- residual: bfloat16 [320, 3584], P(('group', 'expert')), parts along dimension 0, may hold values from -10.5 to 10.5
- norm_gain: float32 [3584], replicated, may hold values from 0.5 to 1.5
- routes: int32 [320, 8], P(('group', 'expert')), parts along dimension 0, may hold values from 0 to 31, all different within a row; in each aligned block of 40 rows (0 to 39, 40 to 79, ...) at most 15 rows name the same one
- gate_scores: float32 [320, 8], P(('group', 'expert')), parts along dimension 0, may hold values from 0.05 to 1
- gate_weight: bfloat16 [32, 3584, 1024], P('expert', None, ('tensor', 'pipe')), may hold values from -0.09375 to 0.09375
- up_weight: bfloat16 [32, 3584, 1024], P('expert', None, ('tensor', 'pipe')), may hold values from -0.09375 to 0.09375
- down_weight: bfloat16 [32, 1024, 3584], P('expert', ('tensor', 'pipe')), may hold values from -0.1875 to 0.1875
Outputs:
- layer_out: bfloat16 [320, 3584], P(('group', 'expert'), ('tensor', 'pipe')), parts along dimension 0
The draws below stay inside these ranges and needn't reach their ends.
There are 2 independent parts, one for each index of `group`. The reference program is written for one: setup_inputs(seed, part) draws one part's arguments, and reference() takes and returns one part's arrays. A program takes and returns all parts, laid end to end along the dimension named above; an argument that names none is the same for every part. Nothing has to cross between parts.
Inputs may be any that keep to these rules, and one draw needn't show every extreme that they name: `routes`: each row names 8 different experts. Within each aligned block of 40 rows (the rows of one index of expert) no expert is named more than 15 times, a bound that some block reaches.
All inputs are finite; a program needn't handle non-finite values.
Results may differ from the reference program's by a relative error of at most 0.013.
Values may be sent and summed in bfloat16 or wider, within the bound.
A program may use at most 128 MiB of HBM per device.

```python
import math
import jax
import jax.numpy as jnp
import numpy as np
from jax import lax

D = 3584
FF_WIN = 1024
EXPERTS = 32
TOP = 8
ROW_DEV = 40
CAP = 15
ROWS = 160
N_TENSOR = 2
N_PIPE = 2


def draw_residual(key, part):
    key = jax.random.fold_in(key, 7)
    first_key = jax.random.fold_in(key, 0)
    columns = jnp.arange(D, dtype=jnp.float32) / (D - 1)
    column_scale = 0.3 * jnp.exp(columns * math.log(5.0))
    base_values = jnp.clip(jax.random.normal(first_key, (ROWS, D), jnp.float32), -4.0, 4.0)
    values = base_values * column_scale[None, :]
    return values.astype(jnp.bfloat16)


def level_of(stream_key, shape, shards, low, top_value):
    factor_of, own = 1.0, jax.random.fold_in(stream_key, 6)
    for axis_at, blocks in shards:
        steps = jnp.exp(jax.random.uniform(jax.random.fold_in(own, axis_at), (blocks,), jnp.float32, low / len(shards), top_value / len(shards)))
        factor_of = factor_of * jnp.repeat(steps, shape[axis_at] // blocks).reshape([-1 if axis == axis_at else 1 for axis in range(len(shape))])
    return factor_of


def assign_block(own_key, own, number, rows, number_of, top, reach, lean):
    order = jax.random.permutation(own_key, number_of)
    crowded, usual = portions_of(number_of, rows * top, reach, lean, True), portions_of(number_of, rows * top, reach, lean, False)
    places = jnp.arange(number_of)

    def named(lengths, rotation):
        used = int((lengths > 0).sum())
        fixed = max(1, used // 4)
        moved = fixed + (places - fixed + rotation * (used - fixed)) % max(1, number_of - fixed)
        return jnp.zeros((number_of,), jnp.int32).at[order[jnp.where(places < fixed, places, moved)]].set(jnp.asarray(lengths, jnp.int32))

    lengths = jnp.where(number % 4 == 0, named(crowded, number // 4), named(usual, number - number // 4 - 1))
    mixed = jax.random.permutation(jax.random.fold_in(own, 3), number_of)
    source_of, receiver = mixed[0:number_of // 2 * 2:2], mixed[1:number_of // 2 * 2:2]
    room = jnp.minimum(lengths[source_of] - 1, reach - lengths[receiver]) // 2
    room = jnp.where((source_of == order[0]) | (receiver == order[0]) | (lengths[receiver] == 0), 0, jnp.maximum(room, 0))
    moved = jax.random.randint(jax.random.fold_in(own, 4), (number_of // 2,), 0, 1 << 20) % (room + 1)
    lengths = lengths.at[source_of].add(-moved).at[receiver].add(moved)
    items = jnp.searchsorted(jnp.cumsum(lengths), jnp.arange(rows * top), side="right").astype(jnp.int32)
    listing = items.reshape(top, rows).T
    listing = listing[jax.random.permutation(jax.random.fold_in(own, 1), rows)]
    rotation = jax.random.randint(jax.random.fold_in(own, 2), (rows, 1), 0, top)
    return jnp.take_along_axis(listing, (jnp.arange(top)[None, :] + rotation) % top, axis=1)


def portions_of(amount, total, bound, lean, full):
    weights = [(1 << 20) // math.isqrt(standing ** lean) + 1 for standing in range(1, amount + 1)]
    largest = bound if full else min(bound, max(-(-total // amount), total * weights[0] // sum(weights)))
    least = 1 if total - largest >= amount - 1 else 0
    given, rest = [largest] + [least] * (amount - 1), total - largest - least * (amount - 1)
    while rest > 0:
        candidates = [i for i in range(1, amount) if given[i] < largest] or [i for i in range(1, amount) if given[i] < bound]
        pool, remaining = sum([weights[i] for i in candidates]), rest
        for i in candidates:
            more = min(bound - given[i], max(1, remaining * weights[i] // pool), rest)
            given[i] = given[i] + more
            rest = rest - more
    return np.array(given)


def bell_draw(own_key, extent, spread, reach, shards=(), kind=jnp.bfloat16):
    values = spread * jax.random.normal(own_key, extent, jnp.float32)
    if shards:
        values = values * level_of(own_key, extent, shards, -0.22, 0.18)
    return jnp.clip(values, -reach, reach).astype(kind)


def setup_inputs(seed: int = 0, part: int = 0) -> dict:
    keys = jax.random.split(jax.random.key(seed), 9)
    part_splits = jax.random.split(jax.random.fold_in(keys[8], part), 9)
    attn_terms = bell_draw(part_splits[0], (N_TENSOR, ROWS, D), 0.5, 4.0, ((0, 2), (1, 4)))
    residual = draw_residual(jax.random.fold_in(jax.random.fold_in(keys[8], part), 71), part)
    norm_gain = jnp.clip(1.0 + 0.1 * jax.random.normal(keys[2], (D,), jnp.float32), 0.5, 1.5)
    routes_keys = jax.random.split(jax.random.fold_in(part_splits[3], 1), ROWS // ROW_DEV)
    routes_turns = jax.random.permutation(jax.random.fold_in(part_splits[3], 3), ROWS // ROW_DEV)
    routes = jax.vmap(lambda own, number: assign_block(jax.random.fold_in(part_splits[3], 2), own, number, ROW_DEV, EXPERTS, TOP, CAP, 2))(routes_keys, routes_turns).reshape((ROWS, TOP))
    gate_scores = jnp.clip(jnp.exp(math.log(1.0) - 2.9957323 * jax.random.uniform(part_splits[4], (ROWS, TOP), jnp.float32) ** level_of(part_splits[4], (ROWS, TOP), ((0, 4),), -0.2, 0.2)), 0.05, 1.0)
    gate_weight = bell_draw(keys[5], (EXPERTS, D, FF_WIN), D ** -0.5, 0.09375, ((0, 4), (2, 4)))
    up_weight = bell_draw(keys[6], (EXPERTS, D, FF_WIN), D ** -0.5, 0.09375, ((0, 4), (2, 4)))
    down_weight = bell_draw(keys[7], (EXPERTS, FF_WIN, D), FF_WIN ** -0.5, 0.1875, ((0, 4), (1, 4)))
    return {"attn_terms": attn_terms, "residual": residual, "norm_gain": norm_gain, "routes": routes, "gate_scores": gate_scores, "gate_weight": gate_weight, "up_weight": up_weight, "down_weight": down_weight}


ROUTE_SCALE = 2.5
NORM_EPS = 1e-06

def reference(attn_terms, residual, norm_gain, routes, gate_scores, gate_weight, up_weight, down_weight):
    attn_sum = lax.optimization_barrier(jnp.sum(attn_terms.astype(jnp.float32), axis=0))
    hidden_state = residual.astype(jnp.float32) + attn_sum
    inv_rms = lax.rsqrt(lax.optimization_barrier(jnp.mean(hidden_state * hidden_state, axis=1, keepdims=True)) + NORM_EPS)
    normed = (hidden_state * inv_rms * norm_gain[None, :]).astype(jnp.bfloat16)
    mix_weight = ROUTE_SCALE * gate_scores / lax.optimization_barrier(jnp.sum(gate_scores, axis=1, keepdims=True))
    blocks = ROWS // ROW_DEV
    block_routes = routes.reshape(blocks, ROW_DEV * TOP)
    onehot = (block_routes[:, :, None] == jnp.arange(EXPERTS, dtype=jnp.int32)[None, None, :]).astype(jnp.int32)
    before = jnp.cumsum(onehot, axis=1) - onehot
    slot_index = lax.optimization_barrier(jnp.sum(before * onehot, axis=2)).astype(jnp.int32)
    position = block_routes * CAP + slot_index
    row_ids = jnp.broadcast_to(jnp.arange(ROWS, dtype=jnp.int32).reshape(blocks, ROW_DEV, 1), (blocks, ROW_DEV, TOP))
    row_ids = row_ids.reshape(blocks, ROW_DEV * TOP)
    block_ids = jnp.broadcast_to(jnp.arange(blocks, dtype=jnp.int32)[:, None], (blocks, ROW_DEV * TOP))
    row_table = jnp.zeros((blocks, EXPERTS * CAP), jnp.int32).at[block_ids, position].set(row_ids)
    row_table = row_table.reshape(blocks, EXPERTS, CAP).transpose(1, 0, 2).reshape(EXPERTS, blocks * CAP)
    group_count = N_TENSOR * N_PIPE
    group_width = FF_WIN // group_count

    def expert_rows(operands):
        table_rows, gate_mat, up_mat, down_mat = operands
        inputs = normed[table_rows]
        gate_sums = jnp.dot(inputs, gate_mat, preferred_element_type=jnp.float32)
        up_sums = jnp.dot(inputs, up_mat, preferred_element_type=jnp.float32)
        expert_hidden = (jax.nn.silu(gate_sums) * up_sums).astype(jnp.bfloat16)
        totals = jnp.zeros((inputs.shape[0], D), jnp.float32)
        for group_index in range(group_count):
            lower = group_index * group_width
            group_out = jnp.dot(expert_hidden[:, lower:lower + group_width], down_mat[lower:lower + group_width, :], preferred_element_type=jnp.float32)
            totals = totals + lax.optimization_barrier(group_out.astype(jnp.bfloat16)).astype(jnp.float32)
        return totals
    expert_out = lax.map(expert_rows, (row_table, gate_weight, up_weight, down_weight))
    row_block = (jnp.arange(ROWS, dtype=jnp.int32) // ROW_DEV)[:, None]
    row_slots = slot_index.reshape(ROWS, TOP)
    picked = expert_out[routes, row_block * CAP + row_slots]
    routed = lax.optimization_barrier(jnp.sum(mix_weight[:, :, None] * picked, axis=1))
    return (hidden_state + routed).astype(jnp.bfloat16)
```

```python
import jax
import jax.numpy as jnp
from jax import lax
from jax.experimental import pallas as pl
from jax.experimental.pallas import tpu as pltpu
from jax.sharding import PartitionSpec as P

EXPERTS = 32
TOP = 8
CAP = 15


ROUTE_SCALE = 2.5
NORM_EPS = 1e-06


def slot_positions(routes):
    row_count, top_count = routes.shape
    flat_routes = routes.reshape(row_count * top_count)
    onehot = (flat_routes[:, None] == jnp.arange(EXPERTS, dtype=jnp.int32)[None, :]).astype(
        jnp.int32
    )
    before = jnp.cumsum(onehot, axis=0) - onehot
    slot_index = jnp.sum(before * onehot, axis=1)
    return (flat_routes * CAP + slot_index).reshape(row_count, top_count)


def shards_general(
    attn_terms, residual, norm_gain, routes, gate_scores, gate_weight, up_weight, down_weight
):
    tensor_count = lax.axis_size("tensor")
    pipe_count = lax.axis_size("pipe")
    group_count = tensor_count * pipe_count
    model_width = residual.shape[1]
    piece_width = model_width // group_count
    tensor_pos = lax.axis_index("tensor")
    pipe_pos = lax.axis_index("pipe")
    group_pos = tensor_pos * pipe_count + pipe_pos
    partial_terms = attn_terms[0].astype(jnp.float32)
    attn_sum = lax.psum(partial_terms.astype(jnp.bfloat16), "tensor").astype(jnp.float32)
    hidden_state = residual.astype(jnp.float32) + attn_sum
    inv_rms = lax.rsqrt(jnp.mean(hidden_state * hidden_state, axis=1, keepdims=True) + NORM_EPS)
    normed = (hidden_state * inv_rms * norm_gain[None, :]).astype(jnp.bfloat16)
    own_state = lax.dynamic_slice_in_dim(hidden_state, group_pos * piece_width, piece_width, 1)
    mix_weight = ROUTE_SCALE * gate_scores / jnp.sum(gate_scores, axis=1, keepdims=True)
    positions = slot_positions(routes)
    slot_total = EXPERTS * CAP
    slot_ids = jnp.arange(slot_total, dtype=jnp.int32)[None, :]
    placement_matrix = jnp.zeros((routes.shape[0], slot_total), jnp.bfloat16)
    for choice_index in range(TOP):
        placement_matrix = placement_matrix + (
            positions[:, choice_index : choice_index + 1] == slot_ids
        ).astype(jnp.bfloat16)
    send_buffer = lax.dot_general(
        placement_matrix, normed, (((0,), (0,)), ((), ())), preferred_element_type=jnp.float32
    )
    send_buffer = send_buffer.astype(jnp.bfloat16).reshape(EXPERTS, CAP, normed.shape[1])
    received = lax.all_to_all(send_buffer, "expert", split_axis=0, concat_axis=1, tiled=True)
    gate_sums = jnp.einsum(
        "erd,edf->erf", received, gate_weight, preferred_element_type=jnp.float32
    )
    up_sums = jnp.einsum("erd,edf->erf", received, up_weight, preferred_element_type=jnp.float32)
    expert_hidden = (jax.nn.silu(gate_sums) * up_sums).astype(jnp.bfloat16)
    partial_out = jnp.einsum(
        "erf,efd->erd", expert_hidden, down_weight, preferred_element_type=jnp.float32
    ).astype(jnp.bfloat16)
    returned = lax.all_to_all(partial_out, "expert", split_axis=1, concat_axis=0, tiled=True)
    flat_rows = returned.reshape(EXPERTS * CAP, returned.shape[2])
    picked = flat_rows[positions]
    weighted = jnp.einsum("rk,rkd->rd", mix_weight, picked.astype(jnp.float32))
    combined = lax.psum_scatter(
        weighted.astype(jnp.bfloat16), ("tensor", "pipe"), scatter_dimension=1, tiled=True
    ).astype(jnp.float32)
    return (own_state + combined).astype(jnp.bfloat16)


MESH = pl.DeviceIdType.MESH


def to_lanes(column):
    rows = column.shape[0]
    wide = jnp.broadcast_to(column, (rows, 128))
    return jnp.concatenate([wide, jnp.zeros((128 - rows, 128), jnp.float32)], axis=0).T


def layer_kernel(
    attn_ref, residual_ref, gain_ref, routes_ref, scores_ref, gate_hbm, up_hbm, down_hbm, out_ref,
    gate_v, up_v, down_v, attn_in, state, gathered, joined, gate_acc, up_acc, hidden_v,
    squares, tiles, mix_v, scale_v,
    pair_send, pair_recv, plane_send, plane_recv, back_send, back_recv,
    weight_sem, attn_sems, square_send, square_recv, tile_send, tile_recv,
    gather_send, gather_recv, pair_ssem, pair_rsem, plane_ssem, plane_rsem, back_ssem, back_rsem,
):
    depth = lax.axis_size("expert")
    z, x, c = lax.axis_index("expert"), lax.axis_index("tensor"), lax.axis_index("pipe")
    experts = gate_v.shape[1]
    rows, piece = state.shape
    sibling, across, corner = {"pipe": 1 - c}, {"tensor": 1 - x}, {"tensor": 1 - x, "pipe": 1 - c}
    beyond = [None] + [{"expert": lax.rem(z + d, depth)} for d in range(1, depth)]
    starts = [
        pl.multiple_of((2 * xx + cc) * piece, 128)
        for xx, cc in ((x, c), (x, 1 - c), (1 - x, c), (1 - x, 1 - c))
    ]

    weight_copies = {}
    for k in range(4):
        cut = pl.ds(starts[k], piece)
        weight_copies["gate", k] = pltpu.make_async_copy(
            gate_hbm.at[:, cut, :], gate_v.at[k], weight_sem.at[0, k]
        )
        weight_copies["up", k] = pltpu.make_async_copy(
            up_hbm.at[:, cut, :], up_v.at[k], weight_sem.at[1, k]
        )
    for k in (3, 2, 1, 0):
        weight_copies["down", k] = pltpu.make_async_copy(
            down_hbm.at[:, :, pl.ds(starts[k], piece)], down_v.at[k], weight_sem.at[2, k]
        )
    for copy in weight_copies.values():
        copy.start()

    barrier = pltpu.get_barrier_semaphore()
    partners = [sibling, across, corner] + beyond[1:]
    for partner in partners:
        pl.semaphore_signal(barrier, inc=1, device_id=partner, device_id_type=MESH)
    pl.semaphore_wait(barrier, len(partners))

    sends = []

    def remote(source, target, send_sem, recv_sem, partner):
        return pltpu.make_async_remote_copy(
            src_ref=source, dst_ref=target, send_sem=send_sem, recv_sem=recv_sem,
            device_id=partner, device_id_type=MESH,
        )

    def send(*args):
        copy = remote(*args)
        copy.start()
        sends.append(copy)
        return copy

    attn_copy = send(
        attn_ref.at[0, :, pl.ds(starts[2], piece)], attn_in, attn_sems.at[0], attn_sems.at[1], across
    )
    own_cut = pl.ds(starts[0], piece)
    partial = residual_ref[:, own_cut].astype(jnp.float32) + attn_ref[0, :, own_cut].astype(jnp.float32)
    attn_copy.wait_recv()
    own_state = partial + attn_in[...].astype(jnp.float32)
    state[...] = own_state
    gathered[0, 0] = (own_state * gain_ref[:, own_cut]).astype(jnp.bfloat16)

    gather_count = [0]

    def gather_copy(source, slot, partner):
        number = gather_count[0]
        gather_count[0] += 1
        d, k = slot
        return send(
            gathered.at[source], gathered.at[slot], gather_send.at[number],
            gather_recv.at[d, k], partner,
        )

    def gather_wait(d, k):
        remote(
            gathered.at[d, k], gathered.at[d, k], gather_send.at[0], gather_recv.at[d, k], sibling
        ).wait_recv()

    for d in range(1, depth):
        gather_copy((0, 0), (depth - d, 0), beyond[d])
    gather_copy((0, 0), (0, 2), across)
    gather_copy((0, 0), (0, 1), sibling)

    squares[0] = to_lanes(jnp.sum(own_state * own_state, axis=1, keepdims=True))[:8]
    square_copies = [
        send(squares.at[0], squares.at[k], square_send.at[k], square_recv.at[k], partner)
        for k, partner in ((1, sibling), (2, across), (3, corner))
    ]
    scores = scores_ref[...]
    mix = ROUTE_SCALE * scores / jnp.sum(scores, axis=1, keepdims=True)
    lanes = lax.broadcasted_iota(jnp.int32, (rows, 128), 1)
    chosen = lax.rem(z * experts + lanes, depth * experts)
    chosen = jnp.where(lanes < depth * experts, chosen, -1)
    weights = jnp.zeros((rows, 128), jnp.float32)
    for choice in range(scores.shape[1]):
        weights = weights + jnp.where(
            routes_ref[:, choice : choice + 1] == chosen, mix[:, choice : choice + 1], 0.0
        )
    turned = to_lanes(weights)
    for copy in square_copies:
        copy.wait_recv()
    total = squares[0] + squares[1] + squares[2] + squares[3]
    inverse = lax.rsqrt(total / (4 * piece) + NORM_EPS)
    for d in range(depth):
        tiles[d, 0, :experts] = turned[d * experts : (d + 1) * experts]
        tiles[d, 0, experts:] = inverse
    tile_copies = [
        send(
            tiles.at[d, 0], tiles.at[depth - d, 1], tile_send.at[d], tile_recv.at[depth - d],
            beyond[d],
        )
        for d in range(1, depth)
    ]

    for d in range(1, depth):
        gather_wait(d, 0)
        gather_copy((d, 0), (d, 2), across)
        gather_copy((d, 0), (d, 1), sibling)

    for copy in tile_copies:
        copy.wait_recv()
    for d in range(depth):
        tile = tiles[d, 0 if d == 0 else 1]
        back = jnp.concatenate([tile, jnp.zeros((128 - 2 * experts, 128), jnp.float32)], axis=0).T
        mix_v[d * rows : (d + 1) * rows] = back[:rows]
        scale_v[d * rows : (d + 1) * rows] = jnp.broadcast_to(
            back[:rows, experts : experts + 1], (rows, 128)
        )

    def join(k):
        joined[k] = jnp.concatenate(
            [gathered[d, k].astype(jnp.float32) for d in range(depth)], axis=0
        ).astype(jnp.bfloat16)

    def project(k):
        join(k)
        weight_copies["gate", k].wait()
        weight_copies["up", k].wait()

        def one_expert(e, carry):
            left = joined[k]
            gate = jnp.dot(left, gate_v[k, e], preferred_element_type=jnp.float32)
            up = jnp.dot(left, up_v[k, e], preferred_element_type=jnp.float32)
            if k > 0:
                gate = gate_acc[e] + gate
                up = up_acc[e] + up
            if k < 3:
                gate_acc[e] = gate
                up_acc[e] = up
            else:
                lane = lax.broadcasted_iota(jnp.int32, (depth * rows, 128), 1)
                weight = jnp.sum(jnp.where(lane == e, mix_v[...], 0.0), axis=1, keepdims=True)
                scale = scale_v[:, :1]
                gate = gate * scale
                up = up * (scale * weight)
                hidden_v[e] = (gate / (1.0 + jnp.exp(-gate)) * up).astype(jnp.bfloat16)
            return carry

        lax.fori_loop(0, experts, one_expert, 0)

    project(0)
    gather_wait(0, 2)
    gather_copy((0, 2), (0, 3), sibling)
    for d in range(depth):
        gather_wait(d, 1)
    project(1)
    for d in range(1, depth):
        gather_wait(d, 2)
        gather_copy((d, 2), (d, 3), sibling)
    project(2)
    for d in range(depth):
        gather_wait(d, 3)
    project(3)

    def contract(k):
        weight_copies["down", k].wait()
        left = jnp.concatenate([hidden_v[e] for e in range(experts)], axis=1)
        right = down_v[k].reshape(experts * down_v.shape[2], piece)
        return jnp.dot(left, right, preferred_element_type=jnp.float32)

    def part(values, d):
        return values[d * rows : (d + 1) * rows]

    pairs = {}
    for index, k in ((0, 3), (1, 1)):
        values = contract(k)
        for d in range(depth):
            pair_send[index, d] = part(values, d).astype(jnp.bfloat16)
        pairs[index] = send(
            pair_send.at[index], pair_recv.at[index], pair_ssem.at[index], pair_rsem.at[index], sibling
        )
        if index == 0:
            values = contract(2)
            pairs[0].wait_recv()
            planes = {}
            for d in list(range(1, depth)) + [0]:
                summed = part(values, d) + pair_recv[0, d].astype(jnp.float32)
                plane_send[d] = summed.astype(jnp.bfloat16)
                planes[d] = send(
                    plane_send.at[d], plane_recv.at[d], plane_ssem.at[d], plane_rsem.at[d], across
                )
    values = contract(0)
    pairs[1].wait_recv()
    backs = []
    for d in range(1, depth):
        planes[d].wait_recv()
        summed = part(values, d) + pair_recv[1, d].astype(jnp.float32)
        summed = summed + plane_recv[d].astype(jnp.float32)
        back_send[d] = summed.astype(jnp.bfloat16)
        backs.append(
            send(
                back_send.at[d], back_recv.at[depth - d], back_ssem.at[d], back_rsem.at[depth - d],
                beyond[d],
            )
        )
    planes[0].wait_recv()
    summed = state[...] + part(values, 0) + pair_recv[1, 0].astype(jnp.float32)
    summed = summed + plane_recv[0].astype(jnp.float32)
    for copy in backs:
        copy.wait_recv()
    for d in range(1, depth):
        summed = summed + back_recv[d].astype(jnp.float32)
    out_ref[...] = summed.astype(jnp.bfloat16)
    for copy in sends:
        copy.wait_send()


def shards_kernel(
    attn_terms, residual, norm_gain, routes, gate_scores, gate_weight, up_weight, down_weight
):
    depth = lax.axis_size("expert")
    rows, width = residual.shape
    piece = width // 4
    experts, _, units = gate_weight.shape
    bf16, f32 = jnp.bfloat16, jnp.float32
    dma = pltpu.SemaphoreType.DMA
    vmem, anywhere = pl.BlockSpec(memory_space=pltpu.VMEM), pl.BlockSpec(memory_space=pl.ANY)
    flops = 6 * depth * rows * experts * width * units
    return pl.pallas_call(
        layer_kernel,
        out_shape=jax.ShapeDtypeStruct((rows, piece), bf16),
        in_specs=[vmem] * 5 + [anywhere] * 3,
        out_specs=vmem,
        scratch_shapes=[
            pltpu.VMEM((4, experts, piece, units), bf16),
            pltpu.VMEM((4, experts, piece, units), bf16),
            pltpu.VMEM((4, experts, units, piece), bf16),
            pltpu.VMEM((rows, piece), bf16),
            pltpu.VMEM((rows, piece), f32),
            pltpu.VMEM((depth, 4, rows, piece), bf16),
            pltpu.VMEM((4, depth * rows, piece), bf16),
            pltpu.VMEM((experts, depth * rows, units), f32),
            pltpu.VMEM((experts, depth * rows, units), f32),
            pltpu.VMEM((experts, depth * rows, units), bf16),
            pltpu.VMEM((4, 8, 128), f32),
            pltpu.VMEM((depth, 2, 2 * experts, 128), f32),
            pltpu.VMEM((depth * rows, 128), f32),
            pltpu.VMEM((depth * rows, 128), f32),
            pltpu.VMEM((2, depth, rows, piece), bf16),
            pltpu.VMEM((2, depth, rows, piece), bf16),
            pltpu.VMEM((depth, rows, piece), bf16),
            pltpu.VMEM((depth, rows, piece), bf16),
            pltpu.VMEM((depth, rows, piece), bf16),
            pltpu.VMEM((depth, rows, piece), bf16),
            dma((3, 4)),
            dma((2,)),
            dma((4,)),
            dma((4,)),
            dma((depth,)),
            dma((depth,)),
            dma((4 * depth,)),
            dma((depth, 4)),
            dma((2,)),
            dma((2,)),
            dma((depth,)),
            dma((depth,)),
            dma((depth,)),
            dma((depth,)),
        ],
        compiler_params=pltpu.CompilerParams(
            collective_id=0, has_side_effects=True, vmem_limit_bytes=62 * 1024 * 1024
        ),
        cost_estimate=pl.CostEstimate(
            flops=flops, bytes_accessed=6 * experts * width * units, transcendentals=0
        ),
        name="routed_layer",
    )(
        attn_terms, residual, norm_gain[None, :], routes, gate_scores,
        gate_weight, up_weight, down_weight,
    )


def shards(attn_terms, residual, *rest):
    four_owners = lax.axis_size("tensor") == 2 and lax.axis_size("pipe") == 2
    small = lax.axis_size("expert") <= 4 and rest[3].shape[0] == 8
    whole_tiles = residual.shape[0] % 8 == 0 and residual.shape[1] % 512 == 0
    if four_owners and small and whole_tiles:
        return shards_kernel(attn_terms, residual, *rest)
    return shards_general(attn_terms, residual, *rest)


def solution(mesh):
    placed = (
        P("tensor", ("group", "expert"), None),
        P(("group", "expert"), None),
        P(),
        P(("group", "expert"), None),
        P(("group", "expert"), None),
        P("expert", None, ("tensor", "pipe")),
        P("expert", None, ("tensor", "pipe")),
        P("expert", ("tensor", "pipe"), None),
    )
    return jax.shard_map(
        shards,
        mesh=mesh,
        in_specs=placed,
        out_specs=P(("group", "expert"), ("tensor", "pipe")),
        check_vma=False,
    )
```

```python
import jax
import jax.numpy as jnp
from jax import lax
from jax.experimental import pallas as pl
from jax.experimental.pallas import tpu as pltpu
from jax.sharding import PartitionSpec as P

EXPERTS = 32
TOP = 8
CAP = 15


ROUTE_SCALE = 2.5
NORM_EPS = 1e-06


def slot_positions(routes):
    row_count, top_count = routes.shape
    flat_routes = routes.reshape(row_count * top_count)
    onehot = (flat_routes[:, None] == jnp.arange(EXPERTS, dtype=jnp.int32)[None, :]).astype(
        jnp.int32
    )
    before = jnp.cumsum(onehot, axis=0) - onehot
    slot_index = jnp.sum(before * onehot, axis=1)
    return (flat_routes * CAP + slot_index).reshape(row_count, top_count)


def shards_general(
    attn_terms, residual, norm_gain, routes, gate_scores, gate_weight, up_weight, down_weight
):
    tensor_count = lax.axis_size("tensor")
    pipe_count = lax.axis_size("pipe")
    group_count = tensor_count * pipe_count
    model_width = residual.shape[1]
    piece_width = model_width // group_count
    tensor_pos = lax.axis_index("tensor")
    pipe_pos = lax.axis_index("pipe")
    group_pos = tensor_pos * pipe_count + pipe_pos
    partial_terms = attn_terms[0].astype(jnp.float32)
    attn_sum = lax.psum(partial_terms.astype(jnp.bfloat16), "tensor").astype(jnp.float32)
    hidden_state = residual.astype(jnp.float32) + attn_sum
    inv_rms = lax.rsqrt(jnp.mean(hidden_state * hidden_state, axis=1, keepdims=True) + NORM_EPS)
    normed = (hidden_state * inv_rms * norm_gain[None, :]).astype(jnp.bfloat16)
    own_state = lax.dynamic_slice_in_dim(hidden_state, group_pos * piece_width, piece_width, 1)
    mix_weight = ROUTE_SCALE * gate_scores / jnp.sum(gate_scores, axis=1, keepdims=True)
    positions = slot_positions(routes)
    slot_total = EXPERTS * CAP
    slot_ids = jnp.arange(slot_total, dtype=jnp.int32)[None, :]
    placement_matrix = jnp.zeros((routes.shape[0], slot_total), jnp.bfloat16)
    for choice_index in range(TOP):
        placement_matrix = placement_matrix + (
            positions[:, choice_index : choice_index + 1] == slot_ids
        ).astype(jnp.bfloat16)
    send_buffer = lax.dot_general(
        placement_matrix, normed, (((0,), (0,)), ((), ())), preferred_element_type=jnp.float32
    )
    send_buffer = send_buffer.astype(jnp.bfloat16).reshape(EXPERTS, CAP, normed.shape[1])
    received = lax.all_to_all(send_buffer, "expert", split_axis=0, concat_axis=1, tiled=True)
    gate_sums = jnp.einsum(
        "erd,edf->erf", received, gate_weight, preferred_element_type=jnp.float32
    )
    up_sums = jnp.einsum("erd,edf->erf", received, up_weight, preferred_element_type=jnp.float32)
    expert_hidden = (jax.nn.silu(gate_sums) * up_sums).astype(jnp.bfloat16)
    partial_out = jnp.einsum(
        "erf,efd->erd", expert_hidden, down_weight, preferred_element_type=jnp.float32
    ).astype(jnp.bfloat16)
    returned = lax.all_to_all(partial_out, "expert", split_axis=1, concat_axis=0, tiled=True)
    flat_rows = returned.reshape(EXPERTS * CAP, returned.shape[2])
    picked = flat_rows[positions]
    weighted = jnp.einsum("rk,rkd->rd", mix_weight, picked.astype(jnp.float32))
    combined = lax.psum_scatter(
        weighted.astype(jnp.bfloat16), ("tensor", "pipe"), scatter_dimension=1, tiled=True
    ).astype(jnp.float32)
    return (own_state + combined).astype(jnp.bfloat16)


MESH = pl.DeviceIdType.MESH


def to_lanes(column):
    rows = column.shape[0]
    wide = jnp.broadcast_to(column, (rows, 128))
    return jnp.concatenate([wide, jnp.zeros((128 - rows, 128), jnp.float32)], axis=0).T


def layer_kernel(
    attn_ref, residual_ref, gain_ref, routes_ref, scores_ref, gate_hbm, up_hbm, down_hbm, out_ref,
    gate_v, up_v, down_v, attn_in, own_in, state, gathered, joined, gate_acc, up_acc, hidden_v,
    squares, tiles, tiles_in, mix_v, scale_v,
    pair_send, pair_recv, plane_send, plane_recv, back_send, back_recv,
    weight_sem, own_sem, attn_sems, square_send, square_recv, tile_send, tile_recv,
    gather_send, gather_recv, pair_ssem, pair_rsem, plane_ssem, plane_rsem, back_ssem, back_rsem,
):
    depth = lax.axis_size("expert")
    z, x, c = lax.axis_index("expert"), lax.axis_index("tensor"), lax.axis_index("pipe")
    experts = gate_v.shape[1]
    rows, piece = state.shape
    sibling, across, corner = {"pipe": 1 - c}, {"tensor": 1 - x}, {"tensor": 1 - x, "pipe": 1 - c}
    beyond = [None] + [{"expert": lax.rem(z + d, depth)} for d in range(1, depth)]
    starts = [
        pl.multiple_of((2 * xx + cc) * piece, 128)
        for xx, cc in ((x, c), (x, 1 - c), (1 - x, c), (1 - x, 1 - c))
    ]

    own_copies = [
        pltpu.make_async_copy(source.at[:, pl.ds(start, piece)], own_in.at[i], own_sem.at[i])
        for i, (source, start) in enumerate(
            ((attn_ref.at[0], starts[2]), (attn_ref.at[0], starts[0]), (residual_ref, starts[0]))
        )
    ]
    for copy in own_copies:
        copy.start()
    weight_copies = {}
    for k in range(4):
        cut = pl.ds(starts[k], piece)
        weight_copies["gate", k] = pltpu.make_async_copy(
            gate_hbm.at[:, cut, :], gate_v.at[k // 2, :, pl.ds(k % 2 * piece, piece)], weight_sem.at[0, k]
        )
        weight_copies["up", k] = pltpu.make_async_copy(
            up_hbm.at[:, cut, :], up_v.at[k // 2, :, pl.ds(k % 2 * piece, piece)], weight_sem.at[1, k]
        )
    for k in (3, 2, 1, 0):
        weight_copies["down", k] = pltpu.make_async_copy(
            down_hbm.at[:, :, pl.ds(starts[k], piece)], down_v.at[k], weight_sem.at[2, k]
        )
    barrier = pltpu.get_barrier_semaphore()
    partners = [sibling, across, corner] + beyond[1:]
    for partner in partners:
        pl.semaphore_signal(barrier, inc=1, device_id=partner, device_id_type=MESH)
    for copy in weight_copies.values():
        copy.start()
    pl.semaphore_wait(barrier, len(partners))

    order = sorted(range(1, depth), key=lambda d: (min(d, depth - d), d))
    arrivals = [depth - d for d in order]
    sends = []

    def remote(source, target, send_sem, recv_sem, partner):
        return pltpu.make_async_remote_copy(
            src_ref=source, dst_ref=target, send_sem=send_sem, recv_sem=recv_sem,
            device_id=partner, device_id_type=MESH,
        )

    def send(*args):
        copy = remote(*args)
        copy.start()
        sends.append(copy)
        return copy

    own_copies[0].wait()
    attn_copy = send(
        own_in.at[0], attn_in, attn_sems.at[0], attn_sems.at[1], across
    )
    own_copies[1].wait()
    own_copies[2].wait()
    gain_rows = piece // 128
    gain = jnp.concatenate(
        [gain_ref[pl.ds((2 * x + c) * gain_rows + i, 1), :] for i in range(gain_rows)], axis=1
    )
    partial = own_in[1].astype(jnp.float32) + own_in[2].astype(jnp.float32)
    attn_copy.wait_recv()
    own_state = partial + attn_in[...].astype(jnp.float32)
    state[...] = own_state
    gathered[0, 0] = (own_state * gain).astype(jnp.bfloat16)

    gather_count = [0]

    def gather_copy(source, slot, partner):
        number = gather_count[0]
        gather_count[0] += 1
        d, k = slot
        return send(
            gathered.at[source], gathered.at[slot], gather_send.at[number],
            gather_recv.at[d, k], partner,
        )

    def gather_wait(d, k):
        remote(
            gathered.at[d, k], gathered.at[d, k], gather_send.at[0], gather_recv.at[d, k], sibling
        ).wait_recv()

    gather_copy((0, 0), (0, 2), across)
    for d in order:
        gather_copy((0, 0), (depth - d, 0), beyond[d])
    gather_copy((0, 0), (0, 1), sibling)

    squares[0] = to_lanes(jnp.sum(own_state * own_state, axis=1, keepdims=True))[:8]
    square_copies = [
        send(squares.at[0], squares.at[k], square_send.at[k], square_recv.at[k], partner)
        for k, partner in ((1, sibling), (2, across), (3, corner))
    ]
    scores = scores_ref[...]
    mix = ROUTE_SCALE * scores / jnp.sum(scores, axis=0, keepdims=True)
    first = lax.broadcasted_iota(jnp.int32, (experts, rows), 0)
    tiles[...] = jnp.zeros_like(tiles)
    for d in range(depth):
        chosen = lax.rem(z + d, depth) * experts + first
        weights = jnp.zeros((experts, rows), jnp.float32)
        for choice in range(scores.shape[0]):
            weights = weights + jnp.where(
                routes_ref[choice : choice + 1, :] == chosen, mix[choice : choice + 1, :], 0.0
            )
        tiles[d, :experts, :rows] = weights
    for copy in square_copies:
        copy.wait_recv()
    total = squares[0] + squares[1] + squares[2] + squares[3]
    inverse = lax.rsqrt(total / (4 * piece) + NORM_EPS)
    for d in range(depth):
        tiles[d, experts:, :] = inverse
    tile_copies = [
        send(
            tiles.at[d], tiles_in.at[depth - d], tile_send.at[d], tile_recv.at[depth - d],
            beyond[d],
        )
        for d in range(1, depth)
    ]

    for d in arrivals:
        gather_wait(d, 0)
        gather_copy((d, 0), (d, 2), across)
        gather_copy((d, 0), (d, 1), sibling)

    def join(half):
        for i in range(2):
            joined[half, :, i * piece : (i + 1) * piece] = jnp.concatenate(
                [gathered[d, 2 * half + i].astype(jnp.float32) for d in range(depth)], axis=0
            ).astype(jnp.bfloat16)

    def project_first(e, carry):
        left = joined[0]
        gate_acc[e] = jnp.dot(left, gate_v[0, e], preferred_element_type=jnp.float32)
        up_acc[e] = jnp.dot(left, up_v[0, e], preferred_element_type=jnp.float32)
        return carry

    def project_last(e, carry):
        left = joined[1]
        lane = lax.broadcasted_iota(jnp.int32, (depth * rows, 128), 1)
        weight = jnp.sum(jnp.where(lane == e, mix_v[...], 0.0), axis=1, keepdims=True)
        scale = scale_v[:, :1]
        gate = gate_acc[e] + jnp.dot(left, gate_v[1, e], preferred_element_type=jnp.float32)
        up = up_acc[e] + jnp.dot(left, up_v[1, e], preferred_element_type=jnp.float32)
        gate = gate * scale
        up = up * (scale * weight)
        hidden_v[e] = (gate / (1.0 + jnp.exp(-gate)) * up).astype(jnp.bfloat16)
        return carry

    def weights_wait(half):
        for k in (2 * half, 2 * half + 1):
            weight_copies["gate", k].wait()
            weight_copies["up", k].wait()

    def forward(d):
        gather_wait(d, 2)
        gather_copy((d, 2), (d, 3), sibling)

    for d in [0] + arrivals:
        gather_wait(d, 1)
    join(0)
    weights_wait(0)
    lax.fori_loop(0, experts // 2, project_first, 0)
    forward(0)
    forward(arrivals[0])
    for copy in tile_copies:
        copy.wait_recv()
    for d in range(depth):
        tile = tiles[d] if d == 0 else tiles_in[d]
        back = jnp.concatenate([tile, jnp.zeros((128 - 2 * experts, 128), jnp.float32)], axis=0).T
        mix_v[d * rows : (d + 1) * rows] = back[:rows]
        scale_v[d * rows : (d + 1) * rows] = jnp.broadcast_to(
            back[:rows, experts : experts + 1], (rows, 128)
        )
    lax.fori_loop(experts // 2, experts, project_first, 0)
    for d in arrivals[1:]:
        forward(d)
    for d in range(depth):
        gather_wait(d, 3)
    join(1)
    weights_wait(1)
    lax.fori_loop(0, experts, project_last, 0)

    def contract(k):
        weight_copies["down", k].wait()
        left = jnp.concatenate([hidden_v[e] for e in range(experts)], axis=1)
        right = down_v[k].reshape(experts * down_v.shape[2], piece)
        return jnp.dot(left, right, preferred_element_type=jnp.float32)

    def part(values, d):
        return values[d * rows : (d + 1) * rows]

    pairs = {}
    for index, k in ((0, 3), (1, 1)):
        values = contract(k)
        for d in range(depth):
            pair_send[index, d] = part(values, d).astype(jnp.bfloat16)
        pairs[index] = send(
            pair_send.at[index], pair_recv.at[index], pair_ssem.at[index], pair_rsem.at[index], sibling
        )
        if index == 0:
            values = contract(2)
            pairs[0].wait_recv()
            planes = {}
            for d in list(range(1, depth)) + [0]:
                summed = part(values, d) + pair_recv[0, d].astype(jnp.float32)
                plane_send[d] = summed.astype(jnp.bfloat16)
                planes[d] = send(
                    plane_send.at[d], plane_recv.at[d], plane_ssem.at[d], plane_rsem.at[d], across
                )
    values = contract(0)
    pairs[1].wait_recv()
    backs = []
    for d in range(1, depth):
        planes[d].wait_recv()
        summed = part(values, d) + pair_recv[1, d].astype(jnp.float32)
        summed = summed + plane_recv[d].astype(jnp.float32)
        back_send[d] = summed.astype(jnp.bfloat16)
        backs.append(
            send(
                back_send.at[d], back_recv.at[depth - d], back_ssem.at[d], back_rsem.at[depth - d],
                beyond[d],
            )
        )
    planes[0].wait_recv()
    summed = state[...] + part(values, 0) + pair_recv[1, 0].astype(jnp.float32)
    summed = summed + plane_recv[0].astype(jnp.float32)
    for copy in backs:
        copy.wait_recv()
    for d in range(1, depth):
        summed = summed + back_recv[d].astype(jnp.float32)
    out_ref[...] = summed.astype(jnp.bfloat16)
    for copy in sends:
        copy.wait_send()


def shards_kernel(
    attn_terms, residual, norm_gain, routes, gate_scores, gate_weight, up_weight, down_weight
):
    depth = lax.axis_size("expert")
    rows, width = residual.shape
    piece = width // 4
    experts, _, units = gate_weight.shape
    bf16, f32 = jnp.bfloat16, jnp.float32
    dma = pltpu.SemaphoreType.DMA
    vmem, anywhere = pl.BlockSpec(memory_space=pltpu.VMEM), pl.BlockSpec(memory_space=pl.ANY)
    flops = 6 * depth * rows * experts * width * units
    return pl.pallas_call(
        layer_kernel,
        out_shape=jax.ShapeDtypeStruct((rows, piece), bf16),
        in_specs=[anywhere] * 2 + [vmem] * 3 + [anywhere] * 3,
        out_specs=vmem,
        scratch_shapes=[
            pltpu.VMEM((2, experts, 2 * piece, units), bf16),
            pltpu.VMEM((2, experts, 2 * piece, units), bf16),
            pltpu.VMEM((4, experts, units, piece), bf16),
            pltpu.VMEM((rows, piece), bf16),
            pltpu.VMEM((3, rows, piece), bf16),
            pltpu.VMEM((rows, piece), f32),
            pltpu.VMEM((depth, 4, rows, piece), bf16),
            pltpu.VMEM((2, depth * rows, 2 * piece), bf16),
            pltpu.VMEM((experts, depth * rows, units), f32),
            pltpu.VMEM((experts, depth * rows, units), f32),
            pltpu.VMEM((experts, depth * rows, units), bf16),
            pltpu.VMEM((4, 8, 128), f32),
            pltpu.VMEM((depth, 2 * experts, 128), f32),
            pltpu.VMEM((depth, 2 * experts, 128), f32),
            pltpu.VMEM((depth * rows, 128), f32),
            pltpu.VMEM((depth * rows, 128), f32),
            pltpu.VMEM((2, depth, rows, piece), bf16),
            pltpu.VMEM((2, depth, rows, piece), bf16),
            pltpu.VMEM((depth, rows, piece), bf16),
            pltpu.VMEM((depth, rows, piece), bf16),
            pltpu.VMEM((depth, rows, piece), bf16),
            pltpu.VMEM((depth, rows, piece), bf16),
            dma((3, 4)),
            dma((3,)),
            dma((2,)),
            dma((4,)),
            dma((4,)),
            dma((depth,)),
            dma((depth,)),
            dma((4 * depth,)),
            dma((depth, 4)),
            dma((2,)),
            dma((2,)),
            dma((depth,)),
            dma((depth,)),
            dma((depth,)),
            dma((depth,)),
        ],
        compiler_params=pltpu.CompilerParams(
            collective_id=0, has_side_effects=True, vmem_limit_bytes=62 * 1024 * 1024
        ),
        cost_estimate=pl.CostEstimate(
            flops=flops, bytes_accessed=6 * experts * width * units, transcendentals=0
        ),
        name="routed_layer",
    )(
        attn_terms, residual, norm_gain.reshape(width // 128, 128), routes.T, gate_scores.T,
        gate_weight, up_weight, down_weight,
    )


def shards(attn_terms, residual, *rest):
    four_owners = lax.axis_size("tensor") == 2 and lax.axis_size("pipe") == 2
    small = lax.axis_size("expert") <= 4 and rest[3].shape[0] == 8
    whole_tiles = residual.shape[0] % 8 == 0 and residual.shape[1] % 512 == 0
    if four_owners and small and whole_tiles:
        return shards_kernel(attn_terms, residual, *rest)
    return shards_general(attn_terms, residual, *rest)


def solution(mesh):
    placed = (
        P("tensor", ("group", "expert"), None),
        P(("group", "expert"), None),
        P(),
        P(("group", "expert"), None),
        P(("group", "expert"), None),
        P("expert", None, ("tensor", "pipe")),
        P("expert", None, ("tensor", "pipe")),
        P("expert", ("tensor", "pipe"), None),
    )
    return jax.shard_map(
        shards,
        mesh=mesh,
        in_specs=placed,
        out_specs=P(("group", "expert"), ("tensor", "pipe")),
        check_vma=False,
    )
```

```python
import jax
import jax.numpy as jnp
from jax import lax
from jax.experimental import pallas as pl
from jax.experimental.pallas import tpu as pltpu
from jax.sharding import PartitionSpec as P

EXPERTS = 32
TOP = 8
CAP = 15


ROUTE_SCALE = 2.5
NORM_EPS = 1e-06


def slot_positions(routes):
    row_count, top_count = routes.shape
    flat_routes = routes.reshape(row_count * top_count)
    onehot = (flat_routes[:, None] == jnp.arange(EXPERTS, dtype=jnp.int32)[None, :]).astype(
        jnp.int32
    )
    before = jnp.cumsum(onehot, axis=0) - onehot
    slot_index = jnp.sum(before * onehot, axis=1)
    return (flat_routes * CAP + slot_index).reshape(row_count, top_count)


def shards_general(
    attn_terms, residual, norm_gain, routes, gate_scores, gate_weight, up_weight, down_weight
):
    tensor_count = lax.axis_size("tensor")
    pipe_count = lax.axis_size("pipe")
    group_count = tensor_count * pipe_count
    model_width = residual.shape[1]
    piece_width = model_width // group_count
    tensor_pos = lax.axis_index("tensor")
    pipe_pos = lax.axis_index("pipe")
    group_pos = tensor_pos * pipe_count + pipe_pos
    partial_terms = attn_terms[0].astype(jnp.float32)
    attn_sum = lax.psum(partial_terms.astype(jnp.bfloat16), "tensor").astype(jnp.float32)
    hidden_state = residual.astype(jnp.float32) + attn_sum
    inv_rms = lax.rsqrt(jnp.mean(hidden_state * hidden_state, axis=1, keepdims=True) + NORM_EPS)
    normed = (hidden_state * inv_rms * norm_gain[None, :]).astype(jnp.bfloat16)
    own_state = lax.dynamic_slice_in_dim(hidden_state, group_pos * piece_width, piece_width, 1)
    mix_weight = ROUTE_SCALE * gate_scores / jnp.sum(gate_scores, axis=1, keepdims=True)
    positions = slot_positions(routes)
    slot_total = EXPERTS * CAP
    slot_ids = jnp.arange(slot_total, dtype=jnp.int32)[None, :]
    placement_matrix = jnp.zeros((routes.shape[0], slot_total), jnp.bfloat16)
    for choice_index in range(TOP):
        placement_matrix = placement_matrix + (
            positions[:, choice_index : choice_index + 1] == slot_ids
        ).astype(jnp.bfloat16)
    send_buffer = lax.dot_general(
        placement_matrix, normed, (((0,), (0,)), ((), ())), preferred_element_type=jnp.float32
    )
    send_buffer = send_buffer.astype(jnp.bfloat16).reshape(EXPERTS, CAP, normed.shape[1])
    received = lax.all_to_all(send_buffer, "expert", split_axis=0, concat_axis=1, tiled=True)
    gate_sums = jnp.einsum(
        "erd,edf->erf", received, gate_weight, preferred_element_type=jnp.float32
    )
    up_sums = jnp.einsum("erd,edf->erf", received, up_weight, preferred_element_type=jnp.float32)
    expert_hidden = (jax.nn.silu(gate_sums) * up_sums).astype(jnp.bfloat16)
    partial_out = jnp.einsum(
        "erf,efd->erd", expert_hidden, down_weight, preferred_element_type=jnp.float32
    ).astype(jnp.bfloat16)
    returned = lax.all_to_all(partial_out, "expert", split_axis=1, concat_axis=0, tiled=True)
    flat_rows = returned.reshape(EXPERTS * CAP, returned.shape[2])
    picked = flat_rows[positions]
    weighted = jnp.einsum("rk,rkd->rd", mix_weight, picked.astype(jnp.float32))
    combined = lax.psum_scatter(
        weighted.astype(jnp.bfloat16), ("tensor", "pipe"), scatter_dimension=1, tiled=True
    ).astype(jnp.float32)
    return (own_state + combined).astype(jnp.bfloat16)


MESH = pl.DeviceIdType.MESH


def to_lanes(column):
    rows = column.shape[0]
    wide = jnp.broadcast_to(column, (rows, 128))
    return jnp.concatenate([wide, jnp.zeros((128 - rows, 128), jnp.float32)], axis=0).T


def layer_kernel(
    attn_ref, residual_ref, gain_ref, routes_ref, scores_ref, gate_hbm, up_hbm, down_hbm, out_ref,
    gate_v, up_v, down_v, attn_in, own_in, state, gathered, joined, gate_acc, up_acc, hidden_v,
    squares, tiles, tiles_in, mix_v, scale_v,
    pair_send, pair_recv, plane_send, plane_recv, back_send, back_recv,
    weight_sem, own_sem, attn_sems, square_send, square_recv, tile_send, tile_recv,
    gather_send, gather_recv, pair_ssem, pair_rsem, plane_ssem, plane_rsem, back_ssem, back_rsem,
):
    depth = lax.axis_size("expert")
    z, x, c = lax.axis_index("expert"), lax.axis_index("tensor"), lax.axis_index("pipe")
    experts = gate_v.shape[1]
    rows, piece = state.shape
    sibling, across, corner = {"pipe": 1 - c}, {"tensor": 1 - x}, {"tensor": 1 - x, "pipe": 1 - c}
    beyond = [None] + [{"expert": lax.rem(z + d, depth)} for d in range(1, depth)]
    starts = [
        pl.multiple_of((2 * xx + cc) * piece, 128)
        for xx, cc in ((x, c), (x, 1 - c), (1 - x, c), (1 - x, 1 - c))
    ]

    own_copies = [
        pltpu.make_async_copy(source.at[:, pl.ds(start, piece)], own_in.at[i], own_sem.at[i])
        for i, (source, start) in enumerate(
            ((attn_ref.at[0], starts[2]), (attn_ref.at[0], starts[0]), (residual_ref, starts[0]))
        )
    ]
    for copy in own_copies:
        copy.start()
    weight_copies = {}
    for k in range(4):
        cut = pl.ds(starts[k], piece)
        weight_copies["gate", k] = pltpu.make_async_copy(
            gate_hbm.at[:, cut, :], gate_v.at[k // 2, :, pl.ds(k % 2 * piece, piece)], weight_sem.at[0, k]
        )
        weight_copies["up", k] = pltpu.make_async_copy(
            up_hbm.at[:, cut, :], up_v.at[k // 2, :, pl.ds(k % 2 * piece, piece)], weight_sem.at[1, k]
        )
    for k in (3, 2, 1, 0):
        weight_copies["down", k] = pltpu.make_async_copy(
            down_hbm.at[:, :, pl.ds(starts[k], piece)], down_v.at[k], weight_sem.at[2, k]
        )
    barrier = pltpu.get_barrier_semaphore()
    partners = [sibling, across, corner] + beyond[1:]
    for partner in partners:
        pl.semaphore_signal(barrier, inc=1, device_id=partner, device_id_type=MESH)
    for copy in weight_copies.values():
        copy.start()
    pl.semaphore_wait(barrier, len(partners))

    order = sorted(range(1, depth), key=lambda d: (min(d, depth - d), d))
    arrivals = [depth - d for d in order]
    sends = []

    def remote(source, target, send_sem, recv_sem, partner):
        return pltpu.make_async_remote_copy(
            src_ref=source, dst_ref=target, send_sem=send_sem, recv_sem=recv_sem,
            device_id=partner, device_id_type=MESH,
        )

    def send(*args):
        copy = remote(*args)
        copy.start()
        sends.append(copy)
        return copy

    own_copies[0].wait()
    attn_copy = send(
        own_in.at[0], attn_in, attn_sems.at[0], attn_sems.at[1], across
    )
    own_copies[1].wait()
    own_copies[2].wait()
    gain_rows = piece // 128
    gain = jnp.concatenate(
        [gain_ref[pl.ds((2 * x + c) * gain_rows + i, 1), :] for i in range(gain_rows)], axis=1
    )
    partial = own_in[1].astype(jnp.float32) + own_in[2].astype(jnp.float32)
    attn_copy.wait_recv()
    own_state = partial + attn_in[...].astype(jnp.float32)
    state[...] = own_state
    gathered[0, 0] = (own_state * gain).astype(jnp.bfloat16)

    gather_count = [0]

    def gather_copy(source, slot, partner):
        number = gather_count[0]
        gather_count[0] += 1
        d, k = slot
        return send(
            gathered.at[source], gathered.at[slot], gather_send.at[number],
            gather_recv.at[d, k], partner,
        )

    def gather_wait(d, k):
        remote(
            gathered.at[d, k], gathered.at[d, k], gather_send.at[0], gather_recv.at[d, k], sibling
        ).wait_recv()

    gather_copy((0, 0), (0, 2), across)
    for d in order:
        gather_copy((0, 0), (depth - d, 0), beyond[d])
    gather_copy((0, 0), (0, 1), sibling)

    squares[0] = to_lanes(jnp.sum(own_state * own_state, axis=1, keepdims=True))[:8]
    square_copies = [
        send(squares.at[0], squares.at[k], square_send.at[k], square_recv.at[k], partner)
        for k, partner in ((1, sibling), (2, across), (3, corner))
    ]
    scores = scores_ref[...]
    mix = ROUTE_SCALE * scores / jnp.sum(scores, axis=0, keepdims=True)
    first = lax.broadcasted_iota(jnp.int32, (experts, rows), 0)
    tiles[...] = jnp.zeros_like(tiles)
    for d in range(depth):
        chosen = lax.rem(z + d, depth) * experts + first
        weights = jnp.zeros((experts, rows), jnp.float32)
        for choice in range(scores.shape[0]):
            weights = weights + jnp.where(
                routes_ref[choice : choice + 1, :] == chosen, mix[choice : choice + 1, :], 0.0
            )
        tiles[d, :experts, :rows] = weights
    for copy in square_copies:
        copy.wait_recv()
    total = squares[0] + squares[1] + squares[2] + squares[3]
    inverse = lax.rsqrt(total / (4 * piece) + NORM_EPS)
    for d in range(depth):
        tiles[d, experts:, :] = inverse
    tile_copies = [
        send(
            tiles.at[d], tiles_in.at[depth - d], tile_send.at[d], tile_recv.at[depth - d],
            beyond[d],
        )
        for d in range(1, depth)
    ]

    for d in arrivals:
        gather_wait(d, 0)
        gather_copy((d, 0), (d, 2), across)
        gather_copy((d, 0), (d, 1), sibling)

    def join(half):
        for i in range(2):
            joined[half, :, i * piece : (i + 1) * piece] = jnp.concatenate(
                [gathered[d, 2 * half + i].astype(jnp.float32) for d in range(depth)], axis=0
            ).astype(jnp.bfloat16)

    def project_first(e, carry):
        left = joined[0]
        gate_acc[e] = jnp.dot(left, gate_v[0, e], preferred_element_type=jnp.float32)
        up_acc[e] = jnp.dot(left, up_v[0, e], preferred_element_type=jnp.float32)
        return carry

    def project_last(e, carry):
        left = joined[1]
        weight = mix_v[:, e : e + 1]
        scale = scale_v[:, :1]
        gate = gate_acc[e] + jnp.dot(left, gate_v[1, e], preferred_element_type=jnp.float32)
        up = up_acc[e] + jnp.dot(left, up_v[1, e], preferred_element_type=jnp.float32)
        gate = gate * scale
        up = up * (scale * weight)
        hidden_v[e] = (gate / (1.0 + jnp.exp(-gate)) * up).astype(jnp.bfloat16)
        return carry

    def weights_wait(half):
        for k in (2 * half, 2 * half + 1):
            weight_copies["gate", k].wait()
            weight_copies["up", k].wait()

    def forward(d):
        gather_wait(d, 2)
        gather_copy((d, 2), (d, 3), sibling)

    for d in [0] + arrivals:
        gather_wait(d, 1)
    join(0)
    weights_wait(0)
    lax.fori_loop(0, experts // 2, project_first, 0, unroll=4)
    forward(0)
    forward(arrivals[0])
    for copy in tile_copies:
        copy.wait_recv()
    for d in range(depth):
        tile = tiles[d] if d == 0 else tiles_in[d]
        back = jnp.concatenate([tile, jnp.zeros((128 - 2 * experts, 128), jnp.float32)], axis=0).T
        mix_v[d * rows : (d + 1) * rows] = back[:rows]
        scale_v[d * rows : (d + 1) * rows] = jnp.broadcast_to(
            back[:rows, experts : experts + 1], (rows, 128)
        )
    lax.fori_loop(experts // 2, experts, project_first, 0, unroll=4)
    for d in arrivals[1:]:
        forward(d)
    for d in range(depth):
        gather_wait(d, 3)
    join(1)
    weights_wait(1)
    for e in range(experts):
        project_last(e, 0)

    def contract(k):
        weight_copies["down", k].wait()
        left = jnp.concatenate([hidden_v[e] for e in range(experts)], axis=1)
        right = down_v[k].reshape(experts * down_v.shape[2], piece)
        return jnp.dot(left, right, preferred_element_type=jnp.float32)

    def part(values, d):
        return values[d * rows : (d + 1) * rows]

    pairs = {}
    for index, k in ((0, 3), (1, 1)):
        values = contract(k)
        for d in range(depth):
            pair_send[index, d] = part(values, d).astype(jnp.bfloat16)
        pairs[index] = send(
            pair_send.at[index], pair_recv.at[index], pair_ssem.at[index], pair_rsem.at[index], sibling
        )
        if index == 0:
            values = contract(2)
            pairs[0].wait_recv()
            planes = {}
            for d in list(range(1, depth)) + [0]:
                summed = part(values, d) + pair_recv[0, d].astype(jnp.float32)
                plane_send[d] = summed.astype(jnp.bfloat16)
                planes[d] = send(
                    plane_send.at[d], plane_recv.at[d], plane_ssem.at[d], plane_rsem.at[d], across
                )
    values = contract(0)
    pairs[1].wait_recv()
    backs = []
    for d in range(1, depth):
        planes[d].wait_recv()
        summed = part(values, d) + pair_recv[1, d].astype(jnp.float32)
        summed = summed + plane_recv[d].astype(jnp.float32)
        back_send[d] = summed.astype(jnp.bfloat16)
        backs.append(
            send(
                back_send.at[d], back_recv.at[depth - d], back_ssem.at[d], back_rsem.at[depth - d],
                beyond[d],
            )
        )
    planes[0].wait_recv()
    summed = state[...] + part(values, 0) + pair_recv[1, 0].astype(jnp.float32)
    summed = summed + plane_recv[0].astype(jnp.float32)
    for copy in backs:
        copy.wait_recv()
    for d in range(1, depth):
        summed = summed + back_recv[d].astype(jnp.float32)
    out_ref[...] = summed.astype(jnp.bfloat16)
    for copy in sends:
        copy.wait_send()


def shards_kernel(
    attn_terms, residual, norm_gain, routes, gate_scores, gate_weight, up_weight, down_weight
):
    depth = lax.axis_size("expert")
    rows, width = residual.shape
    piece = width // 4
    experts, _, units = gate_weight.shape
    bf16, f32 = jnp.bfloat16, jnp.float32
    dma = pltpu.SemaphoreType.DMA
    vmem, anywhere = pl.BlockSpec(memory_space=pltpu.VMEM), pl.BlockSpec(memory_space=pl.ANY)
    flops = 6 * depth * rows * experts * width * units
    return pl.pallas_call(
        layer_kernel,
        out_shape=jax.ShapeDtypeStruct((rows, piece), bf16),
        in_specs=[anywhere] * 2 + [vmem] * 3 + [anywhere] * 3,
        out_specs=vmem,
        scratch_shapes=[
            pltpu.VMEM((2, experts, 2 * piece, units), bf16),
            pltpu.VMEM((2, experts, 2 * piece, units), bf16),
            pltpu.VMEM((4, experts, units, piece), bf16),
            pltpu.VMEM((rows, piece), bf16),
            pltpu.VMEM((3, rows, piece), bf16),
            pltpu.VMEM((rows, piece), f32),
            pltpu.VMEM((depth, 4, rows, piece), bf16),
            pltpu.VMEM((2, depth * rows, 2 * piece), bf16),
            pltpu.VMEM((experts, depth * rows, units), f32),
            pltpu.VMEM((experts, depth * rows, units), f32),
            pltpu.VMEM((experts, depth * rows, units), bf16),
            pltpu.VMEM((4, 8, 128), f32),
            pltpu.VMEM((depth, 2 * experts, 128), f32),
            pltpu.VMEM((depth, 2 * experts, 128), f32),
            pltpu.VMEM((depth * rows, 128), f32),
            pltpu.VMEM((depth * rows, 128), f32),
            pltpu.VMEM((2, depth, rows, piece), bf16),
            pltpu.VMEM((2, depth, rows, piece), bf16),
            pltpu.VMEM((depth, rows, piece), bf16),
            pltpu.VMEM((depth, rows, piece), bf16),
            pltpu.VMEM((depth, rows, piece), bf16),
            pltpu.VMEM((depth, rows, piece), bf16),
            dma((3, 4)),
            dma((3,)),
            dma((2,)),
            dma((4,)),
            dma((4,)),
            dma((depth,)),
            dma((depth,)),
            dma((4 * depth,)),
            dma((depth, 4)),
            dma((2,)),
            dma((2,)),
            dma((depth,)),
            dma((depth,)),
            dma((depth,)),
            dma((depth,)),
        ],
        compiler_params=pltpu.CompilerParams(
            collective_id=0, has_side_effects=True, vmem_limit_bytes=62 * 1024 * 1024
        ),
        cost_estimate=pl.CostEstimate(
            flops=flops, bytes_accessed=6 * experts * width * units, transcendentals=0
        ),
        name="routed_layer",
    )(
        attn_terms, residual, norm_gain.reshape(width // 128, 128), routes.T, gate_scores.T,
        gate_weight, up_weight, down_weight,
    )


def shards(attn_terms, residual, *rest):
    four_owners = lax.axis_size("tensor") == 2 and lax.axis_size("pipe") == 2
    small = lax.axis_size("expert") <= 4 and rest[3].shape[0] == 8
    whole_tiles = residual.shape[0] % 8 == 0 and residual.shape[1] % 512 == 0
    if four_owners and small and whole_tiles:
        return shards_kernel(attn_terms, residual, *rest)
    return shards_general(attn_terms, residual, *rest)


def solution(mesh):
    placed = (
        P("tensor", ("group", "expert"), None),
        P(("group", "expert"), None),
        P(),
        P(("group", "expert"), None),
        P(("group", "expert"), None),
        P("expert", None, ("tensor", "pipe")),
        P("expert", None, ("tensor", "pipe")),
        P("expert", ("tensor", "pipe"), None),
    )
    return jax.shard_map(
        shards,
        mesh=mesh,
        in_specs=placed,
        out_specs=P(("group", "expert"), ("tensor", "pipe")),
        check_vma=False,
    )
```
